32 devices in a mesh: aperture: 16 (over z, y, core), range: 2 (over x).
Axes of the slice: x: 2, y: 2, z: 4, core: 2. Of those that a mesh axis runs over, the one named last changes fastest.
Arguments:
- echoes: bfloat16 [2, 512, 8192], P(None, 'aperture', 'range'), may hold values from -6 to 6
- transmit_chirp: bfloat16 [2, 512], replicated, may hold values from -0.1875 to 0.1875
- band_weights: float32 [4, 2, 2, 512, 16], P(None, None, None, 'aperture'), may hold values from -0.75 to 0.75
- band_offsets: int32 [4, 2, 512], P(None, None, 'aperture'), may hold values from -16 to 16
- band_widths: int32 [4, 2, 512], P(None, None, 'aperture'), may hold values from 8 to 16
- child_rows: int32 [4, 512], P(None, 'aperture'), may hold values from 0 to 15
Outputs:
- subimage: bfloat16 [2, 512, 8192], P(None, 'aperture', 'range')
The draws below stay inside these ranges and needn't reach their ends.
All inputs are finite; a program needn't handle non-finite values.
Results may differ from the reference program's by a relative error of at most 0.007.
Values may be sent and summed in bfloat16 or wider, within the bound.
A program may use at most 128 MiB of HBM per device.

```python
import jax
import jax.numpy as jnp
from jax import lax

RANGE = 8192
P_DEV = 32
TAPS = 512
KERN = 16
SHIFT = 16
LEVELS = 4
PULSES = 512
HALF = 16
N_APERTURE = 16


def with_ends(values, key, low, high):
    place = [jax.random.randint(jax.random.fold_in(key, axis), (), 0, length) for axis, length in enumerate(values.shape)]
    main_axis = values.shape.index(max(values.shape))
    neighbour = place[:main_axis] + [(place[main_axis] + 1) % values.shape[main_axis]] + place[main_axis + 1:]
    return values.at[tuple(place)].set(low).at[tuple(neighbour)].set(high)


def level_of(stream_key, dims, pieces, low, top_value):
    def one(dim, shards_of):
        draws = jax.random.uniform(jax.random.fold_in(jax.random.fold_in(stream_key, 6), dim), (shards_of,), jnp.float32, low / len(pieces), top_value / len(pieces))
        return jnp.repeat(jnp.exp(draws), dims[dim] // shards_of).reshape((-1,) + (1,) * (len(dims) - dim - 1))

    level = one(*pieces[0])
    for cut in pieces[1:]:
        level = level * one(*cut)
    return level


def bell_draw(stream_key, shape, scale, reach, split=(), held_as=jnp.bfloat16):
    drawn = scale * jax.random.normal(stream_key, shape, jnp.float32)
    if split:
        drawn = drawn * level_of(stream_key, shape, split, -0.22, 0.18)
    return jnp.clip(drawn, -reach, reach).astype(held_as)


def setup_inputs(seed: int = 0) -> dict:
    arg_keys = jax.random.split(jax.random.key(seed), 7)
    return {
        "echoes": bell_draw(arg_keys[0], (2, PULSES, RANGE), 1.0, 6.0, ((1, 16), (2, 2))),
        "transmit_chirp": bell_draw(arg_keys[1], (2, TAPS), (2 * TAPS) ** -0.5, 0.1875),
        "band_weights": bell_draw(arg_keys[2], (LEVELS, 2, 2, PULSES, KERN), (4 * KERN) ** -0.5, 0.75, ((3, 16),), jnp.float32),
        "band_offsets": with_ends(jax.random.randint(arg_keys[3], (LEVELS, 2, PULSES), 0 - SHIFT, SHIFT + 1), jax.random.fold_in(arg_keys[3], 1), 0 - SHIFT, SHIFT).astype(jnp.int32),
        "band_widths": with_ends(jax.random.randint(arg_keys[4], (LEVELS, 2, PULSES), KERN // 2, KERN + 1), jax.random.fold_in(arg_keys[4], 1), KERN // 2, KERN).astype(jnp.int32),
        "child_rows": with_ends(jax.random.randint(arg_keys[5], (LEVELS, PULSES), 0, HALF), jax.random.fold_in(arg_keys[5], 1), 0, HALF - 1).astype(jnp.int32),
    }


def compress(padded, transmit_chirp, out_length):
    chirp_values = transmit_chirp.astype(jnp.float32)
    chirp_real = chirp_values[0]
    chirp_imag = chirp_values[1]
    kernel = jnp.stack([jnp.stack([chirp_real, chirp_imag]), jnp.stack([-chirp_imag, chirp_real])])
    result = lax.conv_general_dilated(padded.astype(jnp.float32), kernel, (1,), "VALID",
                                      dimension_numbers=("CNW", "OIW", "CNW"),
                                      precision=lax.Precision.HIGHEST)
    return result[:, :, :out_length]


def shifted_sum(source, kernel, offsets_now, widths_now, child_index, margin, out_length):
    kern_taps = kernel.shape[-1]
    rows_in = source[:, child_index, :]
    starts = (offsets_now + margin - kern_taps // 2).astype(jnp.int32)

    def cut_window(single_row, start_bin):
        return lax.dynamic_slice_in_dim(single_row, start_bin, out_length + kern_taps - 1, 1)

    windows = jax.vmap(cut_window, in_axes=(1, 0), out_axes=1)(rows_in, starts)
    live_taps = (jnp.arange(kern_taps, dtype=jnp.int32)[None, :] < widths_now[:, None]).astype(jnp.float32)
    weights = kernel * live_taps[None]
    real_part = jnp.zeros((windows.shape[1], out_length), jnp.float32)
    imag_part = jnp.zeros((windows.shape[1], out_length), jnp.float32)
    for tap_index in range(kern_taps):
        shifted = windows[:, :, tap_index:tap_index + out_length].astype(jnp.float32)
        weight_real = weights[0, :, tap_index:tap_index + 1]
        weight_imag = weights[1, :, tap_index:tap_index + 1]
        real_part = real_part + weight_real * shifted[0] - weight_imag * shifted[1]
        imag_part = imag_part + weight_real * shifted[1] + weight_imag * shifted[0]
    return jnp.stack([real_part, imag_part])


def merge_rows(lower_child, upper_child, kernel, offsets_now, widths_now, child_index, margin, out_length):
    lower_term = shifted_sum(lower_child, kernel[0], offsets_now[0], widths_now[0], child_index, margin, out_length)
    upper_term = shifted_sum(upper_child, kernel[1], offsets_now[1], widths_now[1], child_index, margin, out_length)
    return lower_term + upper_term


def reference(echoes, transmit_chirp, band_weights, band_offsets, band_widths, child_rows):
    padded = jnp.pad(echoes, ((0, 0), (0, 0), (TAPS // 2, TAPS // 2)))
    blocks = padded.reshape(2, N_APERTURE, P_DEV, RANGE + TAPS).transpose(1, 0, 2, 3)
    compressed = lax.map(lambda block: compress(block, transmit_chirp, RANGE).astype(jnp.bfloat16), blocks)
    subimage = compressed
    margin = SHIFT + KERN // 2
    for level_index in range(LEVELS):
        padded_level = jnp.pad(subimage, ((0, 0), (0, 0), (0, 0), (margin, margin)))

        def one_device(device):
            side_bit = (device >> level_index) & 1
            lower_device = device - side_bit * (1 << level_index)
            upper_device = lower_device + (1 << level_index)
            lower_block = lax.dynamic_index_in_dim(padded_level, lower_device, 0, False)
            upper_block = lax.dynamic_index_in_dim(padded_level, upper_device, 0, False)
            lower_child = lax.dynamic_slice_in_dim(lower_block, side_bit * HALF, HALF, 1)
            upper_child = lax.dynamic_slice_in_dim(upper_block, side_bit * HALF, HALF, 1)
            kernel = lax.dynamic_slice_in_dim(band_weights[level_index], device * P_DEV, P_DEV, 2)
            offsets_now = lax.dynamic_slice_in_dim(band_offsets[level_index], device * P_DEV, P_DEV, 1)
            widths_now = lax.dynamic_slice_in_dim(band_widths[level_index], device * P_DEV, P_DEV, 1)
            child_index = lax.dynamic_slice_in_dim(child_rows[level_index], device * P_DEV, P_DEV, 0)
            merged = merge_rows(lower_child, upper_child, kernel, offsets_now, widths_now, child_index, margin, RANGE)
            return merged.astype(jnp.bfloat16)

        subimage = lax.map(one_device, jnp.arange(N_APERTURE, dtype=jnp.int32))
    return subimage.transpose(1, 0, 2, 3).reshape(2, PULSES, RANGE)
```

```python
import functools

import jax
import jax.numpy as jnp
from jax import lax
from jax.experimental import pallas as pl
from jax.experimental.pallas import tpu as pltpu
from jax.sharding import PartitionSpec as P

KERN = 16
SHIFT = 16
LEVELS = 4
PH = 4
MARGIN = SHIFT + KERN // 2
REACH = MARGIN // PH
STEPS = 2 * REACH + 1
RIM = LEVELS * MARGIN
BLOCK = 256
HALF = 16
PARAMS = pltpu.CompilerParams(vmem_limit_bytes=48 * 1024 * 1024)


def partner(block, axis, stride):
    count = lax.axis_size(axis)
    route = []
    for low in range(count):
        high = low | 1 << stride
        if high != low and high < count:
            route += [(low, high), (high, low)]
    return lax.ppermute(block, axis, route)


def with_halo(cells, axis, dim, width):
    count = lax.axis_size(axis)
    ends = count - 1
    head = lax.slice_in_dim(cells, 0, width, axis=dim)
    tail = lax.slice_in_dim(cells, cells.shape[dim] - width, cells.shape[dim], axis=dim)
    return jnp.concatenate(
        [
            lax.ppermute(tail, axis, [(i, (i + 1) % count) for i in range(ends)]),
            cells,
            lax.ppermute(head, axis, [((i + 1) % count, i) for i in range(ends)]),
        ],
        axis=dim,
    )


def split_store(y, scal_ref, kept_ref, sent_ref):
    row = lax.broadcasted_iota(jnp.int32, y.shape, 0) + scal_ref[0]
    y = jnp.where((row >= 0) & (row < scal_ref[1]), y, 0.0)
    first = y[:, :128]
    second = y[:, 128:]
    upper = scal_ref[2] == 1
    kept_ref[...] = jnp.where(upper, second, first).astype(jnp.bfloat16)
    sent_ref[...] = jnp.where(upper, first, second).astype(jnp.bfloat16)


def compress_kernel(blocks, window, scal_ref, e_ref, t_ref, kept_ref, sent_ref, y_ref):
    rows = BLOCK // PH
    for b in range(blocks):
        w = e_ref[b * BLOCK : b * BLOCK + window, :]
        acc = jnp.dot(t_ref[0], w[:, :64], preferred_element_type=jnp.float32)
        acc = acc + jnp.dot(t_ref[1], w[:, 64:], preferred_element_type=jnp.float32)
        parts = [
            acc[po * rows : (po + 1) * rows, hb * 32 : hb * 32 + 32]
            for hb in range(2)
            for po in range(PH)
        ]
        y_ref[b * rows : (b + 1) * rows, :] = jnp.concatenate(parts, axis=1)
    split_store(y_ref[...], scal_ref, kept_ref, sent_ref)


def merge_kernel(last, out_rows, *refs):
    scal_ref, kept_in, recv_in, wl_ref, off_ref, child_ref = refs[:6]
    if last:
        perm_ref, out_ref, x_ref, y_ref, g_ref, hi_ref, lo_ref = refs[6:]
    else:
        kept_ref, sent_ref, x_ref, y_ref, g_ref, hi_ref, lo_ref = refs[6:]
    rows = kept_in.shape[0]
    x_ref[0:8, :] = jnp.zeros((8, 256), jnp.float32)
    x_ref[rows + 8 : rows + 16, :] = jnp.zeros((8, 256), jnp.float32)
    x_ref[8 : rows + 8, :128] = kept_in[...].astype(jnp.float32)
    x_ref[8 : rows + 8, 128:] = recv_in[...].astype(jnp.float32)
    span = 56
    u = lax.broadcasted_iota(jnp.int32, (span, 256), 0)
    for t in range(2):
        tap = u - MARGIN + KERN // 2 - off_ref[t : t + 1, :]
        for ri in range(2):
            g = jnp.zeros((span, 256), jnp.float32)
            for k in range(KERN):
                g = jnp.where(tap == k, wl_ref[2 * t + ri, k : k + 1, :], g)
            high = g.astype(jnp.bfloat16).astype(jnp.float32)
            g_ref[2 * t + ri] = high
            g_ref[4 + 2 * t + ri] = g - high
    mine = lax.broadcasted_iota(jnp.int32, (HALF, 256), 0) == child_ref[0:1, :]
    for q in range(STEPS):
        for t in range(2):
            for pi in range(PH):
                for ri in range(2):
                    r0 = t * 128 + pi * 32 + ri * 16
                    s = q * PH + pi
                    high = g_ref[2 * t + ri, s : s + 1, :]
                    low = g_ref[4 + 2 * t + ri, s : s + 1, :]
                    hi_ref[q, r0 : r0 + 16, :] = jnp.where(mine, high, 0.0).astype(jnp.bfloat16)
                    lo_ref[q, r0 : r0 + 16, :] = jnp.where(mine, low, 0.0).astype(jnp.bfloat16)
    tile = rows // 2
    for m in range(2):
        acc = jnp.zeros((tile, 256), jnp.float32)
        for q in range(STEPS):
            start = m * tile + 8 - REACH + q
            x = x_ref[start : start + tile, :].astype(jnp.bfloat16)
            acc = acc + jnp.dot(x, hi_ref[q], preferred_element_type=jnp.float32)
            acc = acc + jnp.dot(x, lo_ref[q], preferred_element_type=jnp.float32)
        y_ref[m * tile : (m + 1) * tile, :] = acc
    if not last:
        split_store(y_ref[...], scal_ref, kept_ref, sent_ref)
        return
    for chunk in range(out_rows // 128):
        base = RIM // PH + chunk * 128
        yt = y_ref[base : base + 128, :].T
        for hb in range(2):
            acc = jnp.zeros((32, PH * 128), jnp.float32)
            for po in range(PH):
                r0 = hb * 128 + po * 32
                acc = acc + jnp.dot(
                    yt[r0 : r0 + 32].astype(jnp.bfloat16),
                    perm_ref[po],
                    preferred_element_type=jnp.float32,
                )
            acc = acc.astype(jnp.bfloat16)
            lanes = slice(chunk * PH * 128, (chunk + 1) * PH * 128)
            for ro in range(2):
                out_ref[ro, hb * 16 : hb * 16 + 16, lanes] = acc[ro * 16 : ro * 16 + 16]


def body(echoes, transmit_chirp, band_weights, band_offsets, band_widths, child_rows):
    range_bins = echoes.shape[2]
    taps = transmit_chirp.shape[1]
    halo = taps // 2 + RIM
    blocks = -(-(range_bins + 2 * RIM) // BLOCK)
    rows = blocks * (BLOCK // PH)
    window = BLOCK + taps
    length = blocks * BLOCK + taps
    ap = lax.axis_index("aperture")
    first_row = lax.axis_index("range") * (range_bins // PH) - RIM // PH
    total_rows = range_bins * lax.axis_size("range") // PH

    vm = pl.BlockSpec(memory_space=pltpu.VMEM)
    sm = pl.BlockSpec(memory_space=pltpu.SMEM)
    half_shape = jax.ShapeDtypeStruct((rows, 128), jnp.bfloat16)

    def scalars(level):
        bit = ap >> level & 1
        return jnp.stack([first_row, jnp.int32(total_rows), bit]).astype(jnp.int32)

    padded = with_halo(echoes, "range", 2, halo)
    padded = jnp.pad(padded, ((0, 0), (0, 0), (0, length - padded.shape[2])))
    turned = jnp.stack([padded[1], -padded[0]])
    both = jnp.stack([padded, turned]).reshape(2, 2, 2, HALF, length)
    e_t = both.transpose(0, 2, 1, 3, 4).reshape(128, length).T

    ring = jnp.pad(transmit_chirp, ((0, 0), (0, window + 1 - taps)))
    toep = jnp.tile(ring, (1, BLOCK))[:, : BLOCK * window].reshape(2, BLOCK // PH, PH, window)
    toep = toep.transpose(0, 2, 1, 3).reshape(2, BLOCK, window)

    kept, sent = pl.pallas_call(
        functools.partial(compress_kernel, blocks, window),
        out_shape=(half_shape, half_shape),
        in_specs=[sm, vm, vm],
        out_specs=(vm, vm),
        scratch_shapes=[pltpu.VMEM((rows, 256), jnp.float32)],
        compiler_params=PARAMS,
        name="compress",
    )(scalars(0), e_t, toep)

    side = jnp.stack([ap >> level & 1 for level in range(LEVELS)])
    live = jnp.arange(KERN, dtype=jnp.int32) < band_widths[..., None]
    w = jnp.where(live[:, :, None], band_weights, 0.0)
    w = jnp.where(side[:, None, None, None, None] == 0, w, w[:, ::-1])
    w = w.transpose(0, 1, 2, 4, 3).reshape(LEVELS, 2, 2, KERN, 2, 1, 1, HALF)
    wr, wi = w[:, :, 0], w[:, :, 1]
    wl = jnp.stack(
        [jnp.concatenate([wr, wi], axis=5), jnp.concatenate([-wi, wr], axis=5)], axis=2
    )
    wl = jnp.broadcast_to(wl, (LEVELS, 2, 2, KERN, 2, PH, 2, HALF)).reshape(LEVELS, 4, KERN, 256)
    off = jnp.where(side[:, None, None] == 0, band_offsets, band_offsets[:, ::-1])
    off = off.reshape(LEVELS, 2, 2, 1, 1, HALF) + jnp.arange(PH, dtype=jnp.int32)[:, None, None]
    off = jnp.broadcast_to(off, (LEVELS, 2, 2, PH, 2, HALF)).reshape(LEVELS, 2, 256)
    child = child_rows.reshape(LEVELS, 1, 2, 1, 1, HALF)
    child = jnp.broadcast_to(child, (LEVELS, 1, 2, PH, 2, HALF)).reshape(LEVELS, 1, 256)
    bins = jnp.arange(PH * 128, dtype=jnp.int32)
    perm = (
        bins[None, None, :]
        == PH * jnp.arange(128, dtype=jnp.int32)[None, :, None]
        + jnp.arange(PH, dtype=jnp.int32)[:, None, None]
    ).astype(jnp.bfloat16)

    for level in range(LEVELS):
        received = partner(sent, "aperture", level)
        last = level == LEVELS - 1
        operands = [scalars(level + 1), kept, received, wl[level], off[level], child[level]]
        if last:
            operands.append(perm)
        result = pl.pallas_call(
            functools.partial(merge_kernel, last, range_bins // PH),
            out_shape=jax.ShapeDtypeStruct(echoes.shape, jnp.bfloat16)
            if last
            else (half_shape, half_shape),
            in_specs=[sm] + [vm] * (len(operands) - 1),
            out_specs=vm if last else (vm, vm),
            scratch_shapes=[
                pltpu.VMEM((rows + 16, 256), jnp.float32),
                pltpu.VMEM((rows, 256), jnp.float32),
                pltpu.VMEM((8, 56, 256), jnp.float32),
                pltpu.VMEM((STEPS, 256, 256), jnp.bfloat16),
                pltpu.VMEM((STEPS, 256, 256), jnp.bfloat16),
            ],
            compiler_params=PARAMS,
            name="merge_last" if last else "merge",
        )(*operands)
        if last:
            return result
        kept, sent = result


def solution(mesh):
    return jax.shard_map(
        body,
        mesh=mesh,
        in_specs=(
            P(None, "aperture", "range"),
            P(),
            P(None, None, None, "aperture", None),
            P(None, None, "aperture"),
            P(None, None, "aperture"),
            P(None, "aperture"),
        ),
        out_specs=P(None, "aperture", "range"),
        check_vma=False,
    )
```

```python
import functools

import jax
import jax.numpy as jnp
from jax import lax
from jax.experimental import pallas as pl
from jax.experimental.pallas import tpu as pltpu
from jax.sharding import PartitionSpec as P

KERN = 16
SHIFT = 16
LEVELS = 4
PH = 4
MARGIN = SHIFT + KERN // 2
REACH = MARGIN // PH
STEPS = 2 * REACH + 1
RIM = LEVELS * MARGIN
BLOCK = 256
PIECES = 2
HALF = 16
PARAMS = pltpu.CompilerParams(vmem_limit_bytes=48 * 1024 * 1024)


def partner(block, axis, stride):
    count = lax.axis_size(axis)
    route = []
    for low in range(count):
        high = low | 1 << stride
        if high != low and high < count:
            route += [(low, high), (high, low)]
    return lax.ppermute(block, axis, route)


def with_halo(cells, axis, dim, width):
    count = lax.axis_size(axis)
    ends = count - 1
    head = lax.slice_in_dim(cells, 0, width, axis=dim)
    tail = lax.slice_in_dim(cells, cells.shape[dim] - width, cells.shape[dim], axis=dim)
    return jnp.concatenate(
        [
            lax.ppermute(tail, axis, [(i, (i + 1) % count) for i in range(ends)]),
            cells,
            lax.ppermute(head, axis, [((i + 1) % count, i) for i in range(ends)]),
        ],
        axis=dim,
    )


def split_store(y, scal_ref, kept_ref, sent_ref):
    row = lax.broadcasted_iota(jnp.int32, y.shape, 0) + scal_ref[0]
    y = jnp.where((row >= 0) & (row < scal_ref[1]), y, 0.0)
    first = y[:, :128]
    second = y[:, 128:]
    upper = scal_ref[2] == 1
    kept_ref[...] = jnp.where(upper, second, first).astype(jnp.bfloat16)
    sent_ref[...] = jnp.where(upper, first, second).astype(jnp.bfloat16)


def compress_kernel(start, blocks, window, scal_ref, e_ref, t_ref, kept_ref, sent_ref, y_ref):
    rows = BLOCK // PH
    for b in range(blocks):
        w = e_ref[(start + b) * BLOCK : (start + b) * BLOCK + window, :]
        acc = jnp.dot(t_ref[0], w[:, :64], preferred_element_type=jnp.float32)
        acc = acc + jnp.dot(t_ref[1], w[:, 64:], preferred_element_type=jnp.float32)
        parts = [
            acc[po * rows : (po + 1) * rows, hb * 32 : hb * 32 + 32]
            for hb in range(2)
            for po in range(PH)
        ]
        y_ref[b * rows : (b + 1) * rows, :] = jnp.concatenate(parts, axis=1)
    split_store(y_ref[: kept_ref.shape[0], :], scal_ref, kept_ref, sent_ref)


def merge_kernel(last, out_rows, *refs):
    scal_ref, kept_in, recv_in, wl_ref, off_ref, child_ref = refs[:6]
    if last:
        perm_ref, out_ref, x_ref, y_ref, g_ref, hi_ref, lo_ref = refs[6:]
    else:
        kept_ref, sent_ref, x_ref, y_ref, g_ref, hi_ref, lo_ref = refs[6:]
    rows = kept_in.shape[0]
    x_ref[0:8, :] = jnp.zeros((8, 256), jnp.float32)
    x_ref[rows + 8 : rows + 16, :] = jnp.zeros((8, 256), jnp.float32)
    x_ref[8 : rows + 8, :128] = kept_in[...].astype(jnp.float32)
    x_ref[8 : rows + 8, 128:] = recv_in[...].astype(jnp.float32)
    span = 56
    u = lax.broadcasted_iota(jnp.int32, (span, 256), 0)
    for t in range(2):
        tap = u - MARGIN + KERN // 2 - off_ref[t : t + 1, :]
        for ri in range(2):
            g = jnp.zeros((span, 256), jnp.float32)
            for k in range(KERN):
                g = jnp.where(tap == k, wl_ref[2 * t + ri, k : k + 1, :], g)
            high = g.astype(jnp.bfloat16).astype(jnp.float32)
            g_ref[2 * t + ri] = high
            g_ref[4 + 2 * t + ri] = g - high
    mine = lax.broadcasted_iota(jnp.int32, (HALF, 256), 0) == child_ref[0:1, :]
    for q in range(STEPS):
        for t in range(2):
            for pi in range(PH):
                for ri in range(2):
                    r0 = t * 128 + pi * 32 + ri * 16
                    s = q * PH + pi
                    high = g_ref[2 * t + ri, s : s + 1, :]
                    low = g_ref[4 + 2 * t + ri, s : s + 1, :]
                    hi_ref[q, r0 : r0 + 16, :] = jnp.where(mine, high, 0.0).astype(jnp.bfloat16)
                    lo_ref[q, r0 : r0 + 16, :] = jnp.where(mine, low, 0.0).astype(jnp.bfloat16)
    acc = jnp.zeros((rows, 256), jnp.float32)
    for q in range(STEPS):
        start = 8 - REACH + q
        x = x_ref[start : start + rows, :].astype(jnp.bfloat16)
        acc = acc + jnp.dot(x, hi_ref[q], preferred_element_type=jnp.float32)
        acc = acc + jnp.dot(x, lo_ref[q], preferred_element_type=jnp.float32)
    y_ref[...] = acc
    if not last:
        split_store(y_ref[...], scal_ref, kept_ref, sent_ref)
        return
    for chunk in range(out_rows // 128):
        base = RIM // PH + chunk * 128
        yt = y_ref[base : base + 128, :].T
        for hb in range(2):
            acc = jnp.zeros((32, PH * 128), jnp.float32)
            for po in range(PH):
                r0 = hb * 128 + po * 32
                acc = acc + jnp.dot(
                    yt[r0 : r0 + 32].astype(jnp.bfloat16),
                    perm_ref[po],
                    preferred_element_type=jnp.float32,
                )
            acc = acc.astype(jnp.bfloat16)
            lanes = slice(chunk * PH * 128, (chunk + 1) * PH * 128)
            for ro in range(2):
                out_ref[ro, hb * 16 : hb * 16 + 16, lanes] = acc[ro * 16 : ro * 16 + 16]


def body(echoes, transmit_chirp, band_weights, band_offsets, band_widths, child_rows):
    range_bins = echoes.shape[2]
    taps = transmit_chirp.shape[1]
    halo = taps // 2 + RIM
    piece_bins = range_bins // PIECES
    blocks = -(-(piece_bins + 2 * RIM) // BLOCK)
    rows = (piece_bins + 2 * RIM) // PH
    window = BLOCK + taps
    length = (PIECES - 1) * piece_bins + blocks * BLOCK + taps
    ap = lax.axis_index("aperture")
    first_row = lax.axis_index("range") * (range_bins // PH) - RIM // PH
    total_rows = range_bins * lax.axis_size("range") // PH

    vm = pl.BlockSpec(memory_space=pltpu.VMEM)
    sm = pl.BlockSpec(memory_space=pltpu.SMEM)
    half_shape = jax.ShapeDtypeStruct((rows, 128), jnp.bfloat16)

    def scalars(level, piece):
        bit = ap >> level & 1
        start = first_row + piece * (piece_bins // PH)
        return jnp.stack([start, jnp.int32(total_rows), bit]).astype(jnp.int32)

    padded = with_halo(echoes, "range", 2, halo)
    padded = jnp.pad(padded, ((0, 0), (0, 0), (0, length - padded.shape[2])))
    turned = jnp.stack([padded[1], -padded[0]])
    both = jnp.stack([padded, turned]).reshape(2, 2, 2, HALF, length)
    e_t = both.transpose(0, 2, 1, 3, 4).reshape(128, length).T

    ring = jnp.pad(transmit_chirp, ((0, 0), (0, window + 1 - taps)))
    toep = jnp.tile(ring, (1, BLOCK))[:, : BLOCK * window].reshape(2, BLOCK // PH, PH, window)
    toep = toep.transpose(0, 2, 1, 3).reshape(2, BLOCK, window)

    chains = []
    for piece in range(PIECES):
        kept, sent = pl.pallas_call(
            functools.partial(compress_kernel, piece * (piece_bins // BLOCK), blocks, window),
            out_shape=(half_shape, half_shape),
            in_specs=[sm, vm, vm],
            out_specs=(vm, vm),
            scratch_shapes=[pltpu.VMEM((blocks * (BLOCK // PH), 256), jnp.float32)],
            compiler_params=PARAMS,
            cost_estimate=pl.CostEstimate(
                flops=2 * blocks * BLOCK * window * 2 * 256, bytes_accessed=2**21, transcendentals=0
            ),
            name="compress",
        )(scalars(0, piece), e_t, toep)
        chains.append((kept, partner(sent, "aperture", 0)))

    side = jnp.stack([ap >> level & 1 for level in range(LEVELS)])
    live = jnp.arange(KERN, dtype=jnp.int32) < band_widths[..., None]
    w = jnp.where(live[:, :, None], band_weights, 0.0)
    w = jnp.where(side[:, None, None, None, None] == 0, w, w[:, ::-1])
    w = w.transpose(0, 1, 2, 4, 3).reshape(LEVELS, 2, 2, KERN, 2, 1, 1, HALF)
    wr, wi = w[:, :, 0], w[:, :, 1]
    wl = jnp.stack(
        [jnp.concatenate([wr, wi], axis=5), jnp.concatenate([-wi, wr], axis=5)], axis=2
    )
    wl = jnp.broadcast_to(wl, (LEVELS, 2, 2, KERN, 2, PH, 2, HALF)).reshape(LEVELS, 4, KERN, 256)
    off = jnp.where(side[:, None, None] == 0, band_offsets, band_offsets[:, ::-1])
    off = off.reshape(LEVELS, 2, 2, 1, 1, HALF) + jnp.arange(PH, dtype=jnp.int32)[:, None, None]
    off = jnp.broadcast_to(off, (LEVELS, 2, 2, PH, 2, HALF)).reshape(LEVELS, 2, 256)
    child = child_rows.reshape(LEVELS, 1, 2, 1, 1, HALF)
    child = jnp.broadcast_to(child, (LEVELS, 1, 2, PH, 2, HALF)).reshape(LEVELS, 1, 256)
    bins = jnp.arange(PH * 128, dtype=jnp.int32)
    perm = (
        bins[None, None, :]
        == PH * jnp.arange(128, dtype=jnp.int32)[None, :, None]
        + jnp.arange(PH, dtype=jnp.int32)[:, None, None]
    ).astype(jnp.bfloat16)

    flops = 2 * rows * STEPS * 2 * 256 * 256
    for level in range(LEVELS):
        last = level == LEVELS - 1
        for piece in range(PIECES):
            kept, received = chains[piece]
            operands = [scalars(level + 1, piece), kept, received]
            operands += [wl[level], off[level], child[level]]
            if last:
                operands.append(perm)
            result = pl.pallas_call(
                functools.partial(merge_kernel, last, piece_bins // PH),
                out_shape=jax.ShapeDtypeStruct(echoes.shape[:2] + (piece_bins,), jnp.bfloat16)
                if last
                else (half_shape, half_shape),
                in_specs=[sm] + [vm] * (len(operands) - 1),
                out_specs=vm if last else (vm, vm),
                scratch_shapes=[
                    pltpu.VMEM((rows + 16, 256), jnp.float32),
                    pltpu.VMEM((rows, 256), jnp.float32),
                    pltpu.VMEM((8, 56, 256), jnp.float32),
                    pltpu.VMEM((STEPS, 256, 256), jnp.bfloat16),
                    pltpu.VMEM((STEPS, 256, 256), jnp.bfloat16),
                ],
                compiler_params=PARAMS,
                cost_estimate=pl.CostEstimate(
                    flops=flops, bytes_accessed=2**21, transcendentals=0
                ),
                name="merge_last" if last else "merge",
            )(*operands)
            if last:
                chains[piece] = result
            else:
                kept, sent = result
                chains[piece] = (kept, partner(sent, "aperture", level + 1))
    return jnp.concatenate(chains, axis=2)


def solution(mesh):
    return jax.shard_map(
        body,
        mesh=mesh,
        in_specs=(
            P(None, "aperture", "range"),
            P(),
            P(None, None, None, "aperture", None),
            P(None, None, "aperture"),
            P(None, None, "aperture"),
            P(None, "aperture"),
        ),
        out_specs=P(None, "aperture", "range"),
        check_vma=False,
    )
```

```python
import functools

import jax
import jax.numpy as jnp
from jax import lax
from jax.experimental import pallas as pl
from jax.experimental.pallas import tpu as pltpu
from jax.sharding import PartitionSpec as P

KERN = 16
SHIFT = 16
LEVELS = 4
PH = 4
MARGIN = SHIFT + KERN // 2
REACH = MARGIN // PH
STEPS = 2 * REACH + 1
RIM = LEVELS * MARGIN
BLOCK = 256
PIECES = 2
HALF = 16
PARAMS = pltpu.CompilerParams(vmem_limit_bytes=48 * 1024 * 1024)


def partner(block, axis, stride):
    count = lax.axis_size(axis)
    route = []
    for low in range(count):
        high = low | 1 << stride
        if high != low and high < count:
            route += [(low, high), (high, low)]
    return lax.ppermute(block, axis, route)


def with_halo(cells, axis, dim, width):
    count = lax.axis_size(axis)
    ends = count - 1
    head = lax.slice_in_dim(cells, 0, width, axis=dim)
    tail = lax.slice_in_dim(cells, cells.shape[dim] - width, cells.shape[dim], axis=dim)
    return jnp.concatenate(
        [
            lax.ppermute(tail, axis, [(i, (i + 1) % count) for i in range(ends)]),
            cells,
            lax.ppermute(head, axis, [((i + 1) % count, i) for i in range(ends)]),
        ],
        axis=dim,
    )


def split_store(y, scal_ref, kept_ref, sent_ref):
    row = lax.broadcasted_iota(jnp.int32, y.shape, 0) + scal_ref[0]
    y = jnp.where((row >= 0) & (row < scal_ref[1]), y, 0.0)
    first = y[:, :128]
    second = y[:, 128:]
    upper = scal_ref[2] == 1
    kept_ref[...] = jnp.where(upper, second, first).astype(jnp.bfloat16)
    sent_ref[...] = jnp.where(upper, first, second).astype(jnp.bfloat16)


def compress_kernel(start, blocks, window, scal_ref, e_ref, c_ref, kept_ref, sent_ref, y_ref, t_ref):
    rows = BLOCK // PH
    for ri in range(2):
        ring = jnp.broadcast_to(c_ref[ri : ri + 1, :], (rows, window))
        for po in range(PH):
            turned = pltpu.roll(ring, po, 1, stride=PH, stride_axis=0)
            t_ref[ri, po * rows : (po + 1) * rows, :] = turned.astype(jnp.bfloat16)
    for b in range(blocks):
        w = e_ref[(start + b) * BLOCK : (start + b) * BLOCK + window, :]
        acc = jnp.dot(t_ref[0], w[:, :64], preferred_element_type=jnp.float32)
        acc = acc + jnp.dot(t_ref[1], w[:, 64:], preferred_element_type=jnp.float32)
        parts = [
            acc[po * rows : (po + 1) * rows, hb * 32 : hb * 32 + 32]
            for hb in range(2)
            for po in range(PH)
        ]
        y_ref[b * rows : (b + 1) * rows, :] = jnp.concatenate(parts, axis=1)
    split_store(y_ref[: kept_ref.shape[0], :], scal_ref, kept_ref, sent_ref)


def merge_kernel(last, out_rows, *refs):
    scal_ref, kept_in, recv_in, wl_ref, off_ref, child_ref = refs[:6]
    if last:
        perm_ref, out_ref, x_ref, y_ref, g_ref, hi_ref, lo_ref = refs[6:]
    else:
        kept_ref, sent_ref, x_ref, y_ref, g_ref, hi_ref, lo_ref = refs[6:]
    rows = kept_in.shape[0]
    x_ref[0:8, :] = jnp.zeros((8, 256), jnp.float32)
    x_ref[rows + 8 : rows + 16, :] = jnp.zeros((8, 256), jnp.float32)
    x_ref[8 : rows + 8, :128] = kept_in[...].astype(jnp.float32)
    x_ref[8 : rows + 8, 128:] = recv_in[...].astype(jnp.float32)
    span = 56
    u = lax.broadcasted_iota(jnp.int32, (span, 256), 0)
    for t in range(2):
        tap = u - MARGIN + KERN // 2 - off_ref[t : t + 1, :]
        for ri in range(2):
            g = jnp.zeros((span, 256), jnp.float32)
            for k in range(KERN):
                g = jnp.where(tap == k, wl_ref[2 * t + ri, k : k + 1, :], g)
            high = g.astype(jnp.bfloat16).astype(jnp.float32)
            g_ref[2 * t + ri] = high
            g_ref[4 + 2 * t + ri] = g - high
    mine = lax.broadcasted_iota(jnp.int32, (HALF, 256), 0) == child_ref[0:1, :]
    for q in range(STEPS):
        for t in range(2):
            for pi in range(PH):
                for ri in range(2):
                    r0 = t * 128 + pi * 32 + ri * 16
                    s = q * PH + pi
                    high = g_ref[2 * t + ri, s : s + 1, :]
                    low = g_ref[4 + 2 * t + ri, s : s + 1, :]
                    hi_ref[q, r0 : r0 + 16, :] = jnp.where(mine, high, 0.0).astype(jnp.bfloat16)
                    lo_ref[q, r0 : r0 + 16, :] = jnp.where(mine, low, 0.0).astype(jnp.bfloat16)
    acc = jnp.zeros((rows, 256), jnp.float32)
    for q in range(STEPS):
        start = 8 - REACH + q
        x = x_ref[start : start + rows, :].astype(jnp.bfloat16)
        acc = acc + jnp.dot(x, hi_ref[q], preferred_element_type=jnp.float32)
        acc = acc + jnp.dot(x, lo_ref[q], preferred_element_type=jnp.float32)
    y_ref[...] = acc
    if not last:
        split_store(y_ref[...], scal_ref, kept_ref, sent_ref)
        return
    for chunk in range(out_rows // 128):
        base = RIM // PH + chunk * 128
        yt = y_ref[base : base + 128, :].T
        for hb in range(2):
            acc = jnp.zeros((32, PH * 128), jnp.float32)
            for po in range(PH):
                r0 = hb * 128 + po * 32
                acc = acc + jnp.dot(
                    yt[r0 : r0 + 32].astype(jnp.bfloat16),
                    perm_ref[po],
                    preferred_element_type=jnp.float32,
                )
            acc = acc.astype(jnp.bfloat16)
            lanes = slice(chunk * PH * 128, (chunk + 1) * PH * 128)
            for ro in range(2):
                out_ref[ro, hb * 16 : hb * 16 + 16, lanes] = acc[ro * 16 : ro * 16 + 16]


def body(echoes, transmit_chirp, band_weights, band_offsets, band_widths, child_rows):
    range_bins = echoes.shape[2]
    taps = transmit_chirp.shape[1]
    halo = taps // 2 + RIM
    piece_bins = range_bins // PIECES
    blocks = -(-(piece_bins + 2 * RIM) // BLOCK)
    rows = (piece_bins + 2 * RIM) // PH
    window = BLOCK + taps
    length = (PIECES - 1) * piece_bins + blocks * BLOCK + taps
    ap = lax.axis_index("aperture")
    first_row = lax.axis_index("range") * (range_bins // PH) - RIM // PH
    total_rows = range_bins * lax.axis_size("range") // PH

    vm = pl.BlockSpec(memory_space=pltpu.VMEM)
    sm = pl.BlockSpec(memory_space=pltpu.SMEM)
    half_shape = jax.ShapeDtypeStruct((rows, 128), jnp.bfloat16)

    def scalars(level, piece):
        bit = ap >> level & 1
        start = first_row + piece * (piece_bins // PH)
        return jnp.stack([start, jnp.int32(total_rows), bit]).astype(jnp.int32)

    padded = with_halo(echoes, "range", 2, halo)
    padded = jnp.pad(padded, ((0, 0), (0, 0), (0, length - padded.shape[2])))
    turned = jnp.stack([padded[1], -padded[0]])
    both = jnp.stack([padded, turned]).reshape(2, 2, 2, HALF, length)
    e_t = both.transpose(0, 2, 1, 3, 4).reshape(128, length).T

    ring = jnp.pad(transmit_chirp.astype(jnp.float32), ((0, 0), (0, window - taps)))

    chains = []
    for piece in range(PIECES):
        kept, sent = pl.pallas_call(
            functools.partial(compress_kernel, piece * (piece_bins // BLOCK), blocks, window),
            out_shape=(half_shape, half_shape),
            in_specs=[sm, vm, vm],
            out_specs=(vm, vm),
            scratch_shapes=[
                pltpu.VMEM((blocks * (BLOCK // PH), 256), jnp.float32),
                pltpu.VMEM((2, BLOCK, window), jnp.bfloat16),
            ],
            compiler_params=PARAMS,
            cost_estimate=pl.CostEstimate(
                flops=2 * blocks * BLOCK * window * 2 * 256, bytes_accessed=2**21, transcendentals=0
            ),
            name="compress",
        )(scalars(0, piece), e_t, ring)
        chains.append((kept, partner(sent, "aperture", 0)))

    side = jnp.stack([ap >> level & 1 for level in range(LEVELS)])
    live = jnp.arange(KERN, dtype=jnp.int32) < band_widths[..., None]
    w = jnp.where(live[:, :, None], band_weights, 0.0)
    w = jnp.where(side[:, None, None, None, None] == 0, w, w[:, ::-1])
    w = w.transpose(0, 1, 2, 4, 3).reshape(LEVELS, 2, 2, KERN, 2, 1, 1, HALF)
    wr, wi = w[:, :, 0], w[:, :, 1]
    wl = jnp.stack(
        [jnp.concatenate([wr, wi], axis=5), jnp.concatenate([-wi, wr], axis=5)], axis=2
    )
    wl = jnp.broadcast_to(wl, (LEVELS, 2, 2, KERN, 2, PH, 2, HALF)).reshape(LEVELS, 4, KERN, 256)
    off = jnp.where(side[:, None, None] == 0, band_offsets, band_offsets[:, ::-1])
    off = off.reshape(LEVELS, 2, 2, 1, 1, HALF) + jnp.arange(PH, dtype=jnp.int32)[:, None, None]
    off = jnp.broadcast_to(off, (LEVELS, 2, 2, PH, 2, HALF)).reshape(LEVELS, 2, 256)
    child = child_rows.reshape(LEVELS, 1, 2, 1, 1, HALF)
    child = jnp.broadcast_to(child, (LEVELS, 1, 2, PH, 2, HALF)).reshape(LEVELS, 1, 256)
    bins = jnp.arange(PH * 128, dtype=jnp.int32)
    perm = (
        bins[None, None, :]
        == PH * jnp.arange(128, dtype=jnp.int32)[None, :, None]
        + jnp.arange(PH, dtype=jnp.int32)[:, None, None]
    ).astype(jnp.bfloat16)

    flops = 2 * rows * STEPS * 2 * 256 * 256
    for level in range(LEVELS):
        last = level == LEVELS - 1
        for piece in range(PIECES):
            kept, received = chains[piece]
            operands = [scalars(level + 1, piece), kept, received]
            operands += [wl[level], off[level], child[level]]
            if last:
                operands.append(perm)
            result = pl.pallas_call(
                functools.partial(merge_kernel, last, piece_bins // PH),
                out_shape=jax.ShapeDtypeStruct(echoes.shape[:2] + (piece_bins,), jnp.bfloat16)
                if last
                else (half_shape, half_shape),
                in_specs=[sm] + [vm] * (len(operands) - 1),
                out_specs=vm if last else (vm, vm),
                scratch_shapes=[
                    pltpu.VMEM((rows + 16, 256), jnp.float32),
                    pltpu.VMEM((rows, 256), jnp.float32),
                    pltpu.VMEM((8, 56, 256), jnp.float32),
                    pltpu.VMEM((STEPS, 256, 256), jnp.bfloat16),
                    pltpu.VMEM((STEPS, 256, 256), jnp.bfloat16),
                ],
                compiler_params=PARAMS,
                cost_estimate=pl.CostEstimate(
                    flops=flops, bytes_accessed=2**21, transcendentals=0
                ),
                name="merge_last" if last else "merge",
            )(*operands)
            if last:
                chains[piece] = result
            else:
                kept, sent = result
                chains[piece] = (kept, partner(sent, "aperture", level + 1))
    return jnp.concatenate(chains, axis=2)


def solution(mesh):
    return jax.shard_map(
        body,
        mesh=mesh,
        in_specs=(
            P(None, "aperture", "range"),
            P(),
            P(None, None, None, "aperture", None),
            P(None, None, "aperture"),
            P(None, None, "aperture"),
            P(None, "aperture"),
        ),
        out_specs=P(None, "aperture", "range"),
        check_vma=False,
    )
```
